32 devices in a mesh: wide: 16 (over z, y, x), narrow: 2 (over core).
Axes of the slice: x: 2, y: 2, z: 4, core: 2. Of those that a mesh axis runs over, the one named last changes fastest.
Arguments:
- output_gradient: bfloat16 [1024, 16384], P('wide', 'narrow'), may hold values from -6 to 6
- packed_weight_codes: int32 [49152, 8192], P('wide', 'narrow'), may hold values from 0 to 255
- group_zero_offsets: int32 [384, 16384], P('wide', 'narrow'), may hold values from 0 to 15
- group_scale_table: float32 [384, 16384], P('wide', 'narrow'), may hold values from 0.0004 to 0.004
- channel_aware_scale: float32 [49152], P('wide'), may hold values from 0.5 to 2
- adapter_down_matrix: bfloat16 [49152, 16], P('wide'), may hold values from -1.5 to 1.5
- adapter_up_matrix: bfloat16 [16, 16384], P(None, 'narrow'), may hold values from -0.046875 to 0.046875
Outputs:
- grad_input: bfloat16 [1024, 49152], P('narrow', 'wide')
The draws below stay inside these ranges and needn't reach their ends.
Inputs may be any that keep to these rules, and one draw needn't show every extreme that they name: `packed_weight_codes`: word column 128 * b + i holds the code of output column 2 * 128 * b + i in its value modulo 16 and that of column 2 * 128 * b + 128 + i in its value divided by 16.
All inputs are finite; a program needn't handle non-finite values.
Results may differ from the reference program's by a relative error of at most 0.0048.
Values may be sent and summed in bfloat16 or wider, within the bound.
A program may use at most 512 MiB of HBM per device.

```python
import math
import jax
import jax.numpy as jnp
from jax import lax

MODEL_WIDTH = 16384
INPUT_CHANNELS = 49152
GROUP = 128
HALF = 128
ADAPTER_RANK = 16
TOKENS = 1024


def touch_ends(values, own_key, least, top_value):
    shape = values.shape
    place = [jax.random.randint(jax.random.fold_in(own_key, axis), (), 0, shape[axis]) for axis in range(len(shape))]
    values = values.at[tuple(place)].set(least)
    longest = shape.index(max(shape))
    place[longest] = (place[longest] + 1) % shape[longest]
    return values.at[tuple(place)].set(top_value)


def block_levels(stream_key, shape, cuts, smallest, high):
    level = 1.0
    for axis_at, blocks in cuts:
        heights = jax.random.uniform(jax.random.fold_in(jax.random.fold_in(stream_key, 6), axis_at), (blocks,), jnp.float32, smallest / len(cuts), high / len(cuts))
        level = level * jnp.repeat(jnp.exp(heights), shape[axis_at] // blocks).reshape((-1,) + (1,) * (len(shape) - 1 - axis_at))
    return level


def scatter_about(stream_key, dims, width, most, shards=(), held_as=jnp.bfloat16):
    entries = jax.random.normal(stream_key, dims, jnp.float32) * width
    if len(shards) > 0:
        entries = block_levels(stream_key, dims, shards, -0.22, 0.18) * entries
    return jnp.clip(entries, min=-most, max=most).astype(held_as)


def setup_inputs(seed: int = 0) -> dict:
    seeds = jax.random.split(jax.random.key(seed), 8)
    output_gradient = scatter_about(seeds[0], (TOKENS, MODEL_WIDTH), 1.0, 6.0, ((0, 16), (1, 2)))
    packed_weight_codes = touch_ends(jax.random.randint(seeds[1], (INPUT_CHANNELS, MODEL_WIDTH // 2), 0, 256), jax.random.fold_in(seeds[1], 1), 0, 255).astype(jnp.int32)
    group_zero_offsets = touch_ends(jax.random.randint(seeds[2], (INPUT_CHANNELS // GROUP, MODEL_WIDTH), 0, 16), jax.random.fold_in(seeds[2], 1), 0, 15).astype(jnp.int32)
    group_scale_table = jnp.clip(jnp.exp(math.log(0.004) - 2.3025852 * jax.random.uniform(seeds[3], (INPUT_CHANNELS // GROUP, MODEL_WIDTH), jnp.float32) ** block_levels(seeds[3], (INPUT_CHANNELS // GROUP, MODEL_WIDTH), ((0, 16), (1, 2)), -0.2, 0.2)), 0.0004, 0.004)
    channel_aware_scale = jnp.clip(jnp.exp(math.log(2.0) - 1.3862944 * jax.random.uniform(seeds[4], (INPUT_CHANNELS,), jnp.float32) ** block_levels(seeds[4], (INPUT_CHANNELS,), ((0, 16),), -0.2, 0.2)), 0.5, 2.0)
    adapter_down_matrix = scatter_about(seeds[5], (INPUT_CHANNELS, ADAPTER_RANK), ADAPTER_RANK ** -0.5, 1.5, ((0, 16),))
    adapter_up_matrix = scatter_about(seeds[6], (ADAPTER_RANK, MODEL_WIDTH), MODEL_WIDTH ** -0.5, 0.046875, ((1, 2),))
    return dict(output_gradient=output_gradient, packed_weight_codes=packed_weight_codes, group_zero_offsets=group_zero_offsets, group_scale_table=group_scale_table, channel_aware_scale=channel_aware_scale, adapter_down_matrix=adapter_down_matrix, adapter_up_matrix=adapter_up_matrix)


adapter_gain = 0.5


def unpack(words, zero_rows, scale_rows):
    rows, half_cols = words.shape
    low_codes = words % 16
    high_codes = words // 16
    blocks = half_cols // HALF
    codes = jnp.stack([low_codes.reshape(rows, blocks, HALF), high_codes.reshape(rows, blocks, HALF)], axis=2).reshape(rows, 2 * half_cols)
    groups = rows // GROUP
    shifted = (codes.reshape(groups, GROUP, 2 * half_cols) - zero_rows[:, None, :]).astype(jnp.float32)
    return (shifted * scale_rows[:, None, :]).reshape(rows, 2 * half_cols).astype(jnp.bfloat16)


def reference(output_gradient, packed_weight_codes, group_zero_offsets, group_scale_table, channel_aware_scale, adapter_down_matrix, adapter_up_matrix):
    block = GROUP * 8
    grad_float = output_gradient.astype(jnp.float32)

    def one_block(index):
        start = (index * block).astype(jnp.int32)
        first_group = (index * 8).astype(jnp.int32)
        words = lax.dynamic_slice_in_dim(packed_weight_codes, start, block, 0)
        zero_rows = lax.dynamic_slice_in_dim(group_zero_offsets, first_group, 8, 0)
        scale_rows = lax.dynamic_slice_in_dim(group_scale_table, first_group, 8, 0)
        weight = unpack(words, zero_rows, scale_rows)
        return jnp.dot(grad_float, weight.astype(jnp.float32).T, precision=lax.Precision.HIGHEST)

    parts = lax.map(one_block, jnp.arange(INPUT_CHANNELS // block, dtype=jnp.int32))
    quantized_gradient = jnp.transpose(parts, (1, 0, 2)).reshape(TOKENS, INPUT_CHANNELS)
    adapter_inner_total = jnp.dot(output_gradient, adapter_up_matrix.T, preferred_element_type=jnp.float32)
    adapter_gradient = jnp.dot(adapter_inner_total, adapter_down_matrix.astype(jnp.float32).T, precision=lax.Precision.HIGHEST)
    return (quantized_gradient / channel_aware_scale[None, :] + adapter_gain * adapter_gradient).astype(jnp.bfloat16)
```

```python
import jax
import jax.numpy as jnp
from jax import lax
from jax.experimental import pallas as pl
from jax.experimental.pallas import tpu as pltpu
from jax.sharding import PartitionSpec as P

GROUP = 128
HALF = 128
ROWS = 16
CHUNK = 64
TILE = 256
MESH = pl.DeviceIdType.MESH

adapter_gain = 0.5

CHAINS = {16: (4, 2, 2), 64: (4, 8, 2)}
ORDERS = ((2, 0, 1), (1, 0, 2), (0, 2, 1), (0, 1, 2))


def chain_place(me, i, n):
    lower = 2 * me < n
    low = jnp.where(lower, me, n - 1 - me)
    near = jnp.where(lax.rem(i, 2) == 1, low - lax.div(i + 1, 2), low + lax.div(i, 2))
    place = jnp.where(i <= 2 * low, near, i)
    return jnp.where(lower, place, n - 1 - place)


def earlier(d, e, q, pieces):
    yes = None
    for k in range(min(pieces, len(ORDERS))):
        if ORDERS[k].index(d) < ORDERS[k].index(e):
            hit = lax.rem(q, len(ORDERS)) == k
            yes = hit if yes is None else jnp.logical_or(yes, hit)
    return yes


def sends_per_place(e, chains, pieces):
    total = 0
    for q in range(pieces):
        order = ORDERS[q % len(ORDERS)]
        count = 1
        for d in order[: order.index(e)]:
            count *= chains[d]
        total += count
    return total


def kernel(
    chains, cores, pieces,
    own_ref, codes_ref, zero_ref, scale_ref, divisor_ref, down_ref, up_ref,
    inbox_ref, gathered_ref,
    weight, grads, words, stage, inner, zeros, scales,
    recv_sems, send_sems, own_sem, grads_sem, words_sems, stage_sems, inbox_sems,
):
    wide, core = lax.axis_index("wide"), lax.axis_index("narrow")
    n0, n1, n2 = chains
    strides = (n1 * n2, n2, 1)
    here = (lax.div(wide, n1 * n2), lax.rem(lax.div(wide, n2), n1), lax.rem(wide, n2))
    channels, columns = weight.shape
    plane_pieces = n1 * n2 * pieces
    plane_rows = plane_pieces * ROWS
    own_rows = inbox_ref.shape[1]
    block_rows = min(plane_rows, own_rows)
    blocks = plane_rows // block_rows
    chunks = channels // CHUNK
    tiles = channels // TILE

    def load_words(c, slot):
        return pltpu.make_async_copy(
            codes_ref.at[pl.ds(pl.multiple_of(c * CHUNK, CHUNK), CHUNK), :],
            words.at[slot],
            words_sems.at[slot],
        )

    own_copy = pltpu.make_async_copy(
        own_ref, gathered_ref.at[pl.ds(wide * pieces, pieces)], own_sem
    )
    load_words(0, 0).start()
    own_copy.start()

    barrier = pltpu.get_barrier_semaphore()
    for p in range(1, cores):
        pl.semaphore_signal(
            barrier, inc=1, device_id=(wide, lax.rem(core + p, cores)), device_id_type=MESH
        )
    for e in range(3):
        for step in (1, -1):
            @pl.when((here[e] + step >= 0) & (here[e] + step < chains[e]))
            def _():
                pl.semaphore_signal(
                    barrier, inc=1, device_id=(wide + step * strides[e], core), device_id_type=MESH
                )
    greeted = cores - 1
    for e in range(3):
        greeted = greeted + jnp.where(here[e] > 0, 1, 0) + jnp.where(here[e] < chains[e] - 1, 1, 0)
    pl.semaphore_wait(barrier, greeted)

    def forward(src, index, q, offsets, source):
        for e in range(3):
            if chains[e] == 1:
                continue
            clear = jnp.bool_(True)
            for d in range(3):
                if d != e:
                    met = offsets[d] == 0
                    before = earlier(d, e, q, pieces)
                    clear = clear & (met if before is None else met | before)

            def send(ok, step, sem):
                @pl.when(ok)
                def _():
                    pltpu.make_async_remote_copy(
                        src_ref=src,
                        dst_ref=gathered_ref.at[index],
                        send_sem=send_sems.at[sem],
                        recv_sem=recv_sems.at[index],
                        device_id=(wide + step * strides[e], core),
                        device_id_type=MESH,
                    ).start()

            if chains[e] == 2:
                send(clear & (offsets[e] == 0), 1 - 2 * here[e], 2 * e)
            else:
                send(clear & (source[e] <= here[e]) & (here[e] + 1 < chains[e]), 1, 2 * e)
                send(clear & (source[e] >= here[e]) & (here[e] > 0), -1, 2 * e + 1)

    def start_own(q, _):
        forward(own_ref.at[q], wide * pieces + q, q, (0, 0, 0), here)
        return 0

    lax.fori_loop(0, pieces, start_own, 0)

    def receive(plane, event):
        place, q = lax.div(event, pieces), lax.rem(event, pieces)
        offsets = (plane, lax.div(place, n2), lax.rem(place, n2))
        source = tuple(chain_place(here[d], offsets[d], chains[d]) for d in range(3))
        index = (source[0] * strides[0] + source[1] * strides[1] + source[2]) * pieces + q
        slot = gathered_ref.at[index]
        pltpu.make_async_copy(slot, slot, recv_sems.at[index]).wait()
        forward(slot, index, q, offsets, source)

    def receive_range(plane, low, high):
        def body(event, _):
            receive(plane, event)
            return 0

        lax.fori_loop(low, high, body, 0)

    for k in range(zero_ref.shape[0]):
        zeros[k] = zero_ref[k : k + 1, :].astype(jnp.float32)
        scales[k] = scale_ref[k : k + 1, :]

    first_events = plane_pieces - pieces

    def unpack(c, _):
        slot = lax.rem(c, 2)

        @pl.when(c + 1 < chunks)
        def _():
            load_words(c + 1, 1 - slot).start()

        receive_range(
            0,
            pieces + lax.div(c * first_events, chunks),
            pieces + lax.div((c + 1) * first_events, chunks),
        )
        load_words(c, slot).wait()
        group = lax.div(c * CHUNK, GROUP)
        rows = pl.ds(pl.multiple_of(c * CHUNK, CHUNK), CHUNK)

        def block(b, _):
            packed = words[slot, :, pl.ds(pl.multiple_of(b * HALF, HALF), HALF)]
            for half, codes in enumerate((packed & 15, packed >> 4)):
                at = pl.ds(pl.multiple_of(b * 2 * HALF + half * HALF, HALF), HALF)
                shifted = codes.astype(jnp.float32) - zeros[group, :, at]
                weight[rows, at] = (shifted * scales[group, :, at]).astype(jnp.bfloat16)
            return 0

        lax.fori_loop(0, columns // (2 * HALF), block, 0, unroll=4)
        return 0

    lax.fori_loop(0, chunks, unpack, 0)
    own_copy.wait()

    def stage_done(slot):
        for b in range(blocks):
            part = stage.at[slot, pl.ds(b * block_rows, block_rows)]
            pltpu.make_async_copy(part, part, stage_sems.at[slot, b]).wait()

    def plane_body(g, _):
        plane = chain_place(here[0], g, n0)
        load = pltpu.make_async_copy(
            gathered_ref.at[pl.ds(plane * plane_pieces, plane_pieces)], grads, grads_sem
        )
        load.start()
        load.wait()
        up = up_ref[...]
        sums = lax.dot_general(
            grads[...].reshape(plane_rows, columns),
            jnp.concatenate([up, up], axis=0),
            (((1,), (1,)), ((), ())),
            preferred_element_type=jnp.float32,
        )
        high = sums.astype(jnp.bfloat16)
        rest = (sums - high.astype(jnp.float32)).astype(jnp.bfloat16)
        rank = up_ref.shape[0]
        lane = lax.broadcasted_iota(jnp.int32, sums.shape, 1)
        inner[...] = jnp.where(lane < rank, high.astype(jnp.float32), rest.astype(jnp.float32)).astype(jnp.bfloat16)
        events = jnp.where(g + 1 < n0, plane_pieces, 0)

        def tile_body(j, _):
            receive_range(g + 1, lax.div(j * events, tiles), lax.div((j + 1) * events, tiles))
            count = g * tiles + j
            slot = lax.rem(count, 2)
            at = pl.ds(pl.multiple_of(j * TILE, TILE), TILE)
            main = lax.dot_general(
                grads[...].reshape(plane_rows, columns),
                weight[at, :],
                (((1,), (1,)), ((), ())),
                preferred_element_type=jnp.float32,
            )
            down = down_ref[:, at]
            extra = jnp.dot(
                inner[...], jnp.concatenate([down, down], axis=0), preferred_element_type=jnp.float32
            )

            @pl.when(count >= 2)
            def _():
                stage_done(slot)

            stage[slot] = (main * (1.0 / divisor_ref[:, at]) + adapter_gain * extra).astype(jnp.bfloat16)
            for b in range(blocks):
                row = plane * plane_rows + b * block_rows
                owner = lax.div(row, own_rows)
                src = stage.at[slot, pl.ds(b * block_rows, block_rows)]
                to = pl.ds(pl.multiple_of(lax.rem(row, own_rows), block_rows), block_rows)
                dst = inbox_ref.at[core, to, at]

                @pl.when(owner == core)
                def _():
                    pltpu.make_async_copy(src, dst, stage_sems.at[slot, b]).start()

                @pl.when(owner != core)
                def _():
                    pltpu.make_async_remote_copy(
                        src_ref=src,
                        dst_ref=dst,
                        send_sem=stage_sems.at[slot, b],
                        recv_sem=inbox_sems.at[core],
                        device_id=(wide, owner),
                        device_id_type=MESH,
                    ).start()
            return 0

        lax.fori_loop(0, tiles, tile_body, 0)
        return 0

    lax.fori_loop(0, n0, plane_body, 0)

    stage_done((n0 * tiles - 2) % 2)
    stage_done((n0 * tiles - 1) % 2)
    for p in range(1, cores):
        sender = lax.rem(core + p, cores)
        part = inbox_ref.at[sender]
        pltpu.make_async_copy(part, part, inbox_sems.at[sender]).wait()

    def sent(count, sem):
        part = gathered_ref.at[pl.ds(0, count)]
        pltpu.make_async_copy(part, part, send_sems.at[sem]).wait()

    for e in range(3):
        each = sends_per_place(e, chains, pieces)
        if chains[e] == 2:
            sent(each, 2 * e)
        elif chains[e] > 2:
            for v in range(chains[e]):
                @pl.when(here[e] == v)
                def _():
                    if v + 1 < chains[e]:
                        sent(each * (v + 1), 2 * e)
                    if v > 0:
                        sent(each * (chains[e] - v), 2 * e + 1)


def shards(
    output_gradient,
    packed_weight_codes,
    group_zero_offsets,
    group_scale_table,
    channel_aware_scale,
    adapter_down_matrix,
    adapter_up_matrix,
):
    wide, cores = lax.axis_size("wide"), lax.axis_size("narrow")
    chains = CHAINS.get(wide, (wide, 1, 1))
    rows, columns = output_gradient.shape
    channels = packed_weight_codes.shape[0]
    rank = adapter_up_matrix.shape[0]
    groups = group_scale_table.shape[0]
    pieces = rows // ROWS
    tokens = rows * wide
    own_rows = tokens // cores
    plane_pieces = chains[1] * chains[2] * pieces
    plane_rows = plane_pieces * ROWS
    blocks = plane_rows // min(plane_rows, own_rows)
    dma = pltpu.SemaphoreType.DMA
    any_spec = pl.BlockSpec(memory_space=pl.ANY)
    vmem_spec = pl.BlockSpec(memory_space=pltpu.VMEM)

    def call(*args):
        return kernel(chains, cores, pieces, *args)

    inbox, _ = pl.pallas_call(
        call,
        out_shape=[
            jax.ShapeDtypeStruct((cores, own_rows, channels), jnp.bfloat16),
            jax.ShapeDtypeStruct((wide * pieces, ROWS, columns), jnp.bfloat16),
        ],
        in_specs=[any_spec, any_spec] + [vmem_spec] * 5,
        out_specs=[any_spec, any_spec],
        scratch_shapes=[
            pltpu.VMEM((channels, columns), jnp.bfloat16),
            pltpu.VMEM((plane_pieces, ROWS, columns), jnp.bfloat16),
            pltpu.VMEM((2, CHUNK, columns // 2), jnp.int32),
            pltpu.VMEM((2, plane_rows, TILE), jnp.bfloat16),
            pltpu.VMEM((plane_rows, 2 * rank), jnp.bfloat16),
            pltpu.VMEM((groups, 1, columns), jnp.float32),
            pltpu.VMEM((groups, 1, columns), jnp.float32),
            dma((wide * pieces,)),
            dma((6,)),
            dma,
            dma,
            dma((2,)),
            dma((2, blocks)),
            dma((cores,)),
        ],
        compiler_params=pltpu.CompilerParams(
            collective_id=0, has_side_effects=True, vmem_limit_bytes=60 * 1024 * 1024
        ),
        cost_estimate=pl.CostEstimate(
            flops=2 * tokens * columns * channels,
            bytes_accessed=2 * channels * columns + 6 * tokens * columns,
            transcendentals=0,
        ),
        name="gather_unpack_multiply",
    )(
        output_gradient.reshape(pieces, ROWS, columns),
        packed_weight_codes,
        group_zero_offsets,
        group_scale_table,
        channel_aware_scale.reshape(1, channels),
        adapter_down_matrix.T,
        adapter_up_matrix,
    )
    return jnp.sum(inbox.astype(jnp.float32), axis=0).astype(jnp.bfloat16)


def solution(mesh):
    placed = (
        P("wide", "narrow"),
        P("wide", "narrow"),
        P("wide", "narrow"),
        P("wide", "narrow"),
        P("wide"),
        P("wide", None),
        P(None, "narrow"),
    )
    return jax.shard_map(
        shards, mesh=mesh, in_specs=placed, out_specs=P("narrow", "wide"), check_vma=False
    )
```

```python
import itertools

import jax
import jax.numpy as jnp
from jax import lax
from jax.experimental import pallas as pl
from jax.experimental.pallas import tpu as pltpu
from jax.sharding import PartitionSpec as P

GROUP = 128
HALF = 128
ROWS = 16
CHUNK = 64
WORD_SLOTS = 3
TILE = 256
MESH = pl.DeviceIdType.MESH

adapter_gain = 0.5

CHAINS = {16: (4, 2, 2), 64: (4, 8, 2)}
ORDERS = ((2, 0, 1), (1, 0, 2), (0, 2, 1), (0, 1, 2))


def chain_place(me, i, n):
    lower = 2 * me < n
    low = jnp.where(lower, me, n - 1 - me)
    near = jnp.where(lax.rem(i, 2) == 1, low - lax.div(i + 1, 2), low + lax.div(i, 2))
    place = jnp.where(i <= 2 * low, near, i)
    return jnp.where(lower, place, n - 1 - place)


def earlier(d, e, q, pieces):
    yes = None
    for k in range(min(pieces, len(ORDERS))):
        if ORDERS[k].index(d) < ORDERS[k].index(e):
            hit = lax.rem(q, len(ORDERS)) == k
            yes = hit if yes is None else jnp.logical_or(yes, hit)
    return yes


def arrivals(chains, pieces):
    offsets = list(itertools.product(*map(range, chains)))
    order = sorted(
        ((place, q) for place in offsets[1:] for q in range(pieces)),
        key=lambda event: (sum(event[0]), event[1], event[0]),
    )
    codes = [offsets.index(place) * pieces + q for place, q in order]
    cuts = [
        max([at + 1 for at, (place, _) in enumerate(order) if place[0] <= plane], default=0)
        for plane in range(chains[0])
    ]
    return codes, cuts


def pick(values, at):
    result = jnp.int32(values[0])
    for k in range(1, len(values)):
        result = jnp.where(at == k, jnp.int32(values[k]), result)
    return result


def sends_per_place(e, chains, pieces):
    total = 0
    for q in range(pieces):
        order = ORDERS[q % len(ORDERS)]
        count = 1
        for d in order[: order.index(e)]:
            count *= chains[d]
        total += count
    return total


def kernel(
    chains, cores, pieces,
    own_ref, codes_ref, zero_ref, scale_ref, divisor_ref, down_ref, up_ref,
    inbox_ref, gathered_ref,
    weight, grads, words, stage, inner, zeros, scales,
    recv_sems, send_sems, own_sem, grads_sem, words_sems, stage_sems, inbox_sems,
):
    wide, core = lax.axis_index("wide"), lax.axis_index("narrow")
    n0, n1, n2 = chains
    strides = (n1 * n2, n2, 1)
    here = (lax.div(wide, n1 * n2), lax.rem(lax.div(wide, n2), n1), lax.rem(wide, n2))
    channels, columns = weight.shape
    plane_pieces = n1 * n2 * pieces
    plane_rows = plane_pieces * ROWS
    own_rows = inbox_ref.shape[1]
    block_rows = min(plane_rows, own_rows)
    blocks = plane_rows // block_rows
    chunks = channels // CHUNK
    depth = words.shape[0]
    tiles = channels // TILE

    def load_words(c, slot):
        return pltpu.make_async_copy(
            codes_ref.at[pl.ds(pl.multiple_of(c * CHUNK, CHUNK), CHUNK), :],
            words.at[slot],
            words_sems.at[slot],
        )

    own_copy = pltpu.make_async_copy(
        own_ref, gathered_ref.at[pl.ds(wide * pieces, pieces)], own_sem
    )
    for c in range(depth - 1):
        load_words(c, c).start()
    own_copy.start()

    barrier = pltpu.get_barrier_semaphore()
    for p in range(1, cores):
        pl.semaphore_signal(
            barrier, inc=1, device_id=(wide, lax.rem(core + p, cores)), device_id_type=MESH
        )
    for e in range(3):
        for step in (1, -1):
            @pl.when((here[e] + step >= 0) & (here[e] + step < chains[e]))
            def _():
                pl.semaphore_signal(
                    barrier, inc=1, device_id=(wide + step * strides[e], core), device_id_type=MESH
                )
    greeted = cores - 1
    for e in range(3):
        greeted = greeted + jnp.where(here[e] > 0, 1, 0) + jnp.where(here[e] < chains[e] - 1, 1, 0)
    pl.semaphore_wait(barrier, greeted)

    def forward(src, index, q, offsets, source):
        for e in range(3):
            if chains[e] == 1:
                continue
            clear = jnp.bool_(True)
            for d in range(3):
                if d != e:
                    met = offsets[d] == 0
                    before = earlier(d, e, q, pieces)
                    clear = clear & (met if before is None else met | before)

            def send(ok, step, sem):
                @pl.when(ok)
                def _():
                    pltpu.make_async_remote_copy(
                        src_ref=src,
                        dst_ref=gathered_ref.at[index],
                        send_sem=send_sems.at[sem],
                        recv_sem=recv_sems.at[index],
                        device_id=(wide + step * strides[e], core),
                        device_id_type=MESH,
                    ).start()

            if chains[e] == 2:
                send(clear & (offsets[e] == 0), 1 - 2 * here[e], 2 * e)
            else:
                send(clear & (source[e] <= here[e]) & (here[e] + 1 < chains[e]), 1, 2 * e)
                send(clear & (source[e] >= here[e]) & (here[e] > 0), -1, 2 * e + 1)

    def start_own(q, _):
        forward(own_ref.at[q], wide * pieces + q, q, (0, 0, 0), here)
        return 0

    lax.fori_loop(0, pieces, start_own, 0)

    codes, cuts = arrivals(chains, pieces)
    bits = max(1, (n0 * n1 * n2 * pieces - 1).bit_length())
    per_word = 30 // bits
    packed_codes = [
        sum(code << (bits * k) for k, code in enumerate(codes[at : at + per_word]))
        for at in range(0, len(codes), per_word)
    ]
    first = min(len(codes), cuts[0] + len(codes) // 20)
    done = [max(first, cut) for cut in cuts] + [len(codes)]

    def receive(event, _):
        word = pick(packed_codes, lax.div(event, per_word))
        code = (word >> (lax.rem(event, per_word) * bits)) & ((1 << bits) - 1)
        place, q = lax.div(code, pieces), lax.rem(code, pieces)
        offsets = (lax.div(place, n1 * n2), lax.rem(lax.div(place, n2), n1), lax.rem(place, n2))
        source = tuple(chain_place(here[d], offsets[d], chains[d]) for d in range(3))
        index = (source[0] * strides[0] + source[1] * strides[1] + source[2]) * pieces + q
        slot = gathered_ref.at[index]
        pltpu.make_async_copy(slot, slot, recv_sems.at[index]).wait()
        forward(slot, index, q, offsets, source)
        return 0

    def receive_range(low, high):
        lax.fori_loop(low, high, receive, 0)

    for k in range(zero_ref.shape[0]):
        zeros[k] = zero_ref[k : k + 1, :].astype(jnp.float32)
        scales[k] = scale_ref[k : k + 1, :]

    def unpack(c, _):
        slot = lax.rem(c, depth)

        @pl.when(c + depth - 1 < chunks)
        def _():
            load_words(c + depth - 1, lax.rem(c + depth - 1, depth)).start()

        receive_range(lax.div(c * first, chunks), lax.div((c + 1) * first, chunks))
        load_words(c, slot).wait()
        group = lax.div(c * CHUNK, GROUP)
        rows = pl.ds(pl.multiple_of(c * CHUNK, CHUNK), CHUNK)

        def block(b, _):
            packed = words[slot, :, pl.ds(pl.multiple_of(b * HALF, HALF), HALF)]
            for half, codes in enumerate((packed & 15, packed >> 4)):
                at = pl.ds(pl.multiple_of(b * 2 * HALF + half * HALF, HALF), HALF)
                shifted = codes.astype(jnp.float32) - zeros[group, :, at]
                weight[rows, at] = (shifted * scales[group, :, at]).astype(jnp.bfloat16)
            return 0

        lax.fori_loop(0, columns // (2 * HALF), block, 0, unroll=4)
        return 0

    lax.fori_loop(0, chunks, unpack, 0)
    own_copy.wait()

    def stage_done(slot):
        for b in range(blocks):
            part = stage.at[slot, pl.ds(b * block_rows, block_rows)]
            pltpu.make_async_copy(part, part, stage_sems.at[slot, b]).wait()

    def plane_body(g, _):
        plane = chain_place(here[0], g, n0)
        load = pltpu.make_async_copy(
            gathered_ref.at[pl.ds(plane * plane_pieces, plane_pieces)], grads, grads_sem
        )
        load.start()
        load.wait()
        up = up_ref[...]
        sums = lax.dot_general(
            grads[...].reshape(plane_rows, columns),
            jnp.concatenate([up, up], axis=0),
            (((1,), (1,)), ((), ())),
            preferred_element_type=jnp.float32,
        )
        high = sums.astype(jnp.bfloat16)
        rest = (sums - high.astype(jnp.float32)).astype(jnp.bfloat16)
        rank = up_ref.shape[0]
        lane = lax.broadcasted_iota(jnp.int32, sums.shape, 1)
        inner[...] = jnp.where(lane < rank, high.astype(jnp.float32), rest.astype(jnp.float32)).astype(jnp.bfloat16)
        low, events = pick(done, g), pick(done, g + 1) - pick(done, g)

        def tile_body(j, _):
            receive_range(low + lax.div(j * events, tiles), low + lax.div((j + 1) * events, tiles))
            count = g * tiles + j
            slot = lax.rem(count, 2)
            at = pl.ds(pl.multiple_of(j * TILE, TILE), TILE)
            main = lax.dot_general(
                grads[...].reshape(plane_rows, columns),
                weight[at, :],
                (((1,), (1,)), ((), ())),
                preferred_element_type=jnp.float32,
            )
            down = down_ref[:, at]
            extra = jnp.dot(
                inner[...], jnp.concatenate([down, down], axis=0), preferred_element_type=jnp.float32
            )

            @pl.when(count >= 2)
            def _():
                stage_done(slot)

            stage[slot] = (main * (1.0 / divisor_ref[:, at]) + adapter_gain * extra).astype(jnp.bfloat16)
            for b in range(blocks):
                row = plane * plane_rows + b * block_rows
                owner = lax.div(row, own_rows)
                src = stage.at[slot, pl.ds(b * block_rows, block_rows)]
                to = pl.ds(pl.multiple_of(lax.rem(row, own_rows), block_rows), block_rows)
                dst = inbox_ref.at[core, to, at]

                @pl.when(owner == core)
                def _():
                    pltpu.make_async_copy(src, dst, stage_sems.at[slot, b]).start()

                @pl.when(owner != core)
                def _():
                    pltpu.make_async_remote_copy(
                        src_ref=src,
                        dst_ref=dst,
                        send_sem=stage_sems.at[slot, b],
                        recv_sem=inbox_sems.at[core],
                        device_id=(wide, owner),
                        device_id_type=MESH,
                    ).start()
            return 0

        lax.fori_loop(0, tiles, tile_body, 0)
        return 0

    lax.fori_loop(0, n0, plane_body, 0)

    stage_done((n0 * tiles - 2) % 2)
    stage_done((n0 * tiles - 1) % 2)
    for p in range(1, cores):
        sender = lax.rem(core + p, cores)
        part = inbox_ref.at[sender]
        pltpu.make_async_copy(part, part, inbox_sems.at[sender]).wait()

    def sent(count, sem):
        part = gathered_ref.at[pl.ds(0, count)]
        pltpu.make_async_copy(part, part, send_sems.at[sem]).wait()

    for e in range(3):
        each = sends_per_place(e, chains, pieces)
        if chains[e] == 2:
            sent(each, 2 * e)
        elif chains[e] > 2:
            for v in range(chains[e]):
                @pl.when(here[e] == v)
                def _():
                    if v + 1 < chains[e]:
                        sent(each * (v + 1), 2 * e)
                    if v > 0:
                        sent(each * (chains[e] - v), 2 * e + 1)


def shards(
    output_gradient,
    packed_weight_codes,
    group_zero_offsets,
    group_scale_table,
    channel_aware_scale,
    adapter_down_matrix,
    adapter_up_matrix,
):
    wide, cores = lax.axis_size("wide"), lax.axis_size("narrow")
    chains = CHAINS.get(wide, (wide, 1, 1))
    rows, columns = output_gradient.shape
    channels = packed_weight_codes.shape[0]
    rank = adapter_up_matrix.shape[0]
    groups = group_scale_table.shape[0]
    pieces = rows // ROWS
    tokens = rows * wide
    own_rows = tokens // cores
    plane_pieces = chains[1] * chains[2] * pieces
    plane_rows = plane_pieces * ROWS
    blocks = plane_rows // min(plane_rows, own_rows)
    dma = pltpu.SemaphoreType.DMA
    any_spec = pl.BlockSpec(memory_space=pl.ANY)
    vmem_spec = pl.BlockSpec(memory_space=pltpu.VMEM)

    def call(*args):
        return kernel(chains, cores, pieces, *args)

    inbox, _ = pl.pallas_call(
        call,
        out_shape=[
            jax.ShapeDtypeStruct((cores, own_rows, channels), jnp.bfloat16),
            jax.ShapeDtypeStruct((wide * pieces, ROWS, columns), jnp.bfloat16),
        ],
        in_specs=[any_spec, any_spec] + [vmem_spec] * 5,
        out_specs=[any_spec, any_spec],
        scratch_shapes=[
            pltpu.VMEM((channels, columns), jnp.bfloat16),
            pltpu.VMEM((plane_pieces, ROWS, columns), jnp.bfloat16),
            pltpu.VMEM((WORD_SLOTS, CHUNK, columns // 2), jnp.int32),
            pltpu.VMEM((2, plane_rows, TILE), jnp.bfloat16),
            pltpu.VMEM((plane_rows, 2 * rank), jnp.bfloat16),
            pltpu.VMEM((groups, 1, columns), jnp.float32),
            pltpu.VMEM((groups, 1, columns), jnp.float32),
            dma((wide * pieces,)),
            dma((6,)),
            dma,
            dma,
            dma((WORD_SLOTS,)),
            dma((2, blocks)),
            dma((cores,)),
        ],
        compiler_params=pltpu.CompilerParams(
            collective_id=0, has_side_effects=True, vmem_limit_bytes=60 * 1024 * 1024
        ),
        cost_estimate=pl.CostEstimate(
            flops=2 * tokens * columns * channels,
            bytes_accessed=2 * channels * columns + 6 * tokens * columns,
            transcendentals=0,
        ),
        name="gather_unpack_multiply",
    )(
        output_gradient.reshape(pieces, ROWS, columns),
        packed_weight_codes,
        group_zero_offsets,
        group_scale_table,
        channel_aware_scale.reshape(1, channels),
        adapter_down_matrix.T,
        adapter_up_matrix,
    )
    total = inbox[0].astype(jnp.float32)
    for p in range(1, cores):
        total = total + inbox[p].astype(jnp.float32)
    return total.astype(jnp.bfloat16)


def solution(mesh):
    placed = (
        P("wide", "narrow"),
        P("wide", "narrow"),
        P("wide", "narrow"),
        P("wide", "narrow"),
        P("wide"),
        P("wide", None),
        P(None, "narrow"),
    )
    return jax.shard_map(
        shards, mesh=mesh, in_specs=placed, out_specs=P("narrow", "wide"), check_vma=False
    )
```

```python
import itertools

import jax
import jax.numpy as jnp
from jax import lax
from jax.experimental import pallas as pl
from jax.experimental.pallas import tpu as pltpu
from jax.sharding import PartitionSpec as P

GROUP = 128
HALF = 128
ROWS = 16
CHUNK = 64
WORD_SLOTS = 3
TILE = 512
VMEM_BYTES = 60 * 1024 * 1024 + 512 * 1024
MESH = pl.DeviceIdType.MESH

adapter_gain = 0.5

CHAINS = {16: (4, 2, 2), 64: (4, 8, 2)}
ORDERS = ((2, 0, 1), (1, 0, 2), (0, 2, 1), (0, 1, 2))


def chain_place(me, i, n):
    lower = 2 * me < n
    low = jnp.where(lower, me, n - 1 - me)
    near = jnp.where(lax.rem(i, 2) == 1, low - lax.div(i + 1, 2), low + lax.div(i, 2))
    place = jnp.where(i <= 2 * low, near, i)
    return jnp.where(lower, place, n - 1 - place)


def earlier(d, e, q, pieces):
    yes = None
    for k in range(min(pieces, len(ORDERS))):
        if ORDERS[k].index(d) < ORDERS[k].index(e):
            hit = lax.rem(q, len(ORDERS)) == k
            yes = hit if yes is None else jnp.logical_or(yes, hit)
    return yes


def arrivals(chains, pieces):
    offsets = list(itertools.product(*map(range, chains)))
    order = sorted(
        ((place, q) for place in offsets[1:] for q in range(pieces)),
        key=lambda event: (sum(event[0]), event[1], event[0]),
    )
    codes = [offsets.index(place) * pieces + q for place, q in order]
    cuts = [
        max([at + 1 for at, (place, _) in enumerate(order) if place[0] <= plane], default=0)
        for plane in range(chains[0])
    ]
    return codes, cuts


def pick(values, at):
    result = jnp.int32(values[0])
    for k in range(1, len(values)):
        result = jnp.where(at == k, jnp.int32(values[k]), result)
    return result


def sends_per_place(e, chains, pieces):
    total = 0
    for q in range(pieces):
        order = ORDERS[q % len(ORDERS)]
        count = 1
        for d in order[: order.index(e)]:
            count *= chains[d]
        total += count
    return total


def kernel(
    chains, cores, pieces,
    own_ref, codes_ref, zero_hbm, scale_hbm, up_hbm, divisor_ref, down_ref,
    inbox_ref, gathered_ref,
    weight, grads, words, stage, inner, zeros, scales, zero_ref, scale_ref, up_ref,
    recv_sems, send_sems, own_sem, table_sems, grads_sem, words_sems, stage_sems, inbox_sems,
):
    wide, core = lax.axis_index("wide"), lax.axis_index("narrow")
    n0, n1, n2 = chains
    strides = (n1 * n2, n2, 1)
    here = (lax.div(wide, n1 * n2), lax.rem(lax.div(wide, n2), n1), lax.rem(wide, n2))
    channels, columns = weight.shape
    plane_pieces = n1 * n2 * pieces
    plane_rows = plane_pieces * ROWS
    own_rows = inbox_ref.shape[1]
    block_rows = min(plane_rows, own_rows)
    blocks = plane_rows // block_rows
    chunks = channels // CHUNK
    depth = words.shape[0]
    tile = stage.shape[2]
    tiles = channels // tile

    def load_words(c, slot):
        return pltpu.make_async_copy(
            codes_ref.at[pl.ds(pl.multiple_of(c * CHUNK, CHUNK), CHUNK), :],
            words.at[slot],
            words_sems.at[slot],
        )

    own_copy = pltpu.make_async_copy(
        own_ref, gathered_ref.at[pl.ds(wide * pieces, pieces)], own_sem
    )
    for c in range(depth - 1):
        load_words(c, c).start()
    own_copy.start()
    tables = [
        pltpu.make_async_copy(src, dst, table_sems.at[k])
        for k, (src, dst) in enumerate(
            ((zero_hbm, zero_ref), (scale_hbm, scale_ref), (up_hbm, up_ref))
        )
    ]
    for table in tables:
        table.start()

    barrier = pltpu.get_barrier_semaphore()
    for p in range(1, cores):
        pl.semaphore_signal(
            barrier, inc=1, device_id=(wide, lax.rem(core + p, cores)), device_id_type=MESH
        )
    for e in range(3):
        for step in (1, -1):
            @pl.when((here[e] + step >= 0) & (here[e] + step < chains[e]))
            def _():
                pl.semaphore_signal(
                    barrier, inc=1, device_id=(wide + step * strides[e], core), device_id_type=MESH
                )
    greeted = cores - 1
    for e in range(3):
        greeted = greeted + jnp.where(here[e] > 0, 1, 0) + jnp.where(here[e] < chains[e] - 1, 1, 0)
    pl.semaphore_wait(barrier, greeted)

    def forward(src, index, q, offsets, source):
        for e in range(3):
            if chains[e] == 1:
                continue
            clear = jnp.bool_(True)
            for d in range(3):
                if d != e:
                    met = offsets[d] == 0
                    before = earlier(d, e, q, pieces)
                    clear = clear & (met if before is None else met | before)

            def send(ok, step, sem):
                @pl.when(ok)
                def _():
                    pltpu.make_async_remote_copy(
                        src_ref=src,
                        dst_ref=gathered_ref.at[index],
                        send_sem=send_sems.at[sem],
                        recv_sem=recv_sems.at[index],
                        device_id=(wide + step * strides[e], core),
                        device_id_type=MESH,
                    ).start()

            if chains[e] == 2:
                send(clear & (offsets[e] == 0), 1 - 2 * here[e], 2 * e)
            else:
                send(clear & (source[e] <= here[e]) & (here[e] + 1 < chains[e]), 1, 2 * e)
                send(clear & (source[e] >= here[e]) & (here[e] > 0), -1, 2 * e + 1)

    def start_own(q, _):
        forward(own_ref.at[q], wide * pieces + q, q, (0, 0, 0), here)
        return 0

    lax.fori_loop(0, pieces, start_own, 0)

    codes, cuts = arrivals(chains, pieces)
    bits = max(1, (n0 * n1 * n2 * pieces - 1).bit_length())
    per_word = 30 // bits
    packed_codes = [
        sum(code << (bits * k) for k, code in enumerate(codes[at : at + per_word]))
        for at in range(0, len(codes), per_word)
    ]
    first = min(len(codes), cuts[0] + len(codes) // 20)
    done = [max(first, cut) for cut in cuts] + [len(codes)]

    def receive(event, _):
        word = pick(packed_codes, lax.div(event, per_word))
        code = (word >> (lax.rem(event, per_word) * bits)) & ((1 << bits) - 1)
        place, q = lax.div(code, pieces), lax.rem(code, pieces)
        offsets = (lax.div(place, n1 * n2), lax.rem(lax.div(place, n2), n1), lax.rem(place, n2))
        source = tuple(chain_place(here[d], offsets[d], chains[d]) for d in range(3))
        index = (source[0] * strides[0] + source[1] * strides[1] + source[2]) * pieces + q
        slot = gathered_ref.at[index]
        pltpu.make_async_copy(slot, slot, recv_sems.at[index]).wait()
        forward(slot, index, q, offsets, source)
        return 0

    def receive_range(low, high):
        lax.fori_loop(low, high, receive, 0)

    for table in tables:
        table.wait()
    for k in range(zero_ref.shape[0]):
        zeros[k] = zero_ref[k : k + 1, :].astype(jnp.float32)
        scales[k] = scale_ref[k : k + 1, :]

    def unpack(c, _):
        slot = lax.rem(c, depth)

        @pl.when(c + depth - 1 < chunks)
        def _():
            load_words(c + depth - 1, lax.rem(c + depth - 1, depth)).start()

        receive_range(lax.div(c * first, chunks), lax.div((c + 1) * first, chunks))
        load_words(c, slot).wait()
        group = lax.div(c * CHUNK, GROUP)
        rows = pl.ds(pl.multiple_of(c * CHUNK, CHUNK), CHUNK)

        def block(b, _):
            packed = words[slot, :, pl.ds(pl.multiple_of(b * HALF, HALF), HALF)]
            for half, codes in enumerate((packed & 15, packed >> 4)):
                at = pl.ds(pl.multiple_of(b * 2 * HALF + half * HALF, HALF), HALF)
                shifted = codes.astype(jnp.float32) - zeros[group, :, at]
                weight[rows, at] = (shifted * scales[group, :, at]).astype(jnp.bfloat16)
            return 0

        lax.fori_loop(0, columns // (2 * HALF), block, 0, unroll=4)
        return 0

    lax.fori_loop(0, chunks, unpack, 0)
    own_copy.wait()

    def stage_done(slot):
        for b in range(blocks):
            part = stage.at[slot, pl.ds(b * block_rows, block_rows)]
            pltpu.make_async_copy(part, part, stage_sems.at[slot, b]).wait()

    def plane_body(g, _):
        plane = chain_place(here[0], g, n0)
        load = pltpu.make_async_copy(
            gathered_ref.at[pl.ds(plane * plane_pieces, plane_pieces)], grads, grads_sem
        )
        load.start()
        load.wait()
        up = up_ref[...]
        sums = lax.dot_general(
            grads[...].reshape(plane_rows, columns),
            jnp.concatenate([up, up], axis=0),
            (((1,), (1,)), ((), ())),
            preferred_element_type=jnp.float32,
        )
        high = sums.astype(jnp.bfloat16)
        rest = (sums - high.astype(jnp.float32)).astype(jnp.bfloat16)
        rank = up_ref.shape[0]
        lane = lax.broadcasted_iota(jnp.int32, sums.shape, 1)
        inner[...] = jnp.where(lane < rank, high.astype(jnp.float32), rest.astype(jnp.float32)).astype(jnp.bfloat16)
        low, events = pick(done, g), pick(done, g + 1) - pick(done, g)

        def tile_body(j, _):
            receive_range(low + lax.div(j * events, tiles), low + lax.div((j + 1) * events, tiles))
            count = g * tiles + j
            slot = lax.rem(count, 2)
            at = pl.ds(pl.multiple_of(j * tile, tile), tile)
            main = lax.dot_general(
                weight[at, :],
                grads[...].reshape(plane_rows, columns),
                (((1,), (1,)), ((), ())),
                preferred_element_type=jnp.float32,
            ).T
            down = down_ref[:, at]
            extra = jnp.dot(
                inner[...], jnp.concatenate([down, down], axis=0), preferred_element_type=jnp.float32
            )

            @pl.when(count >= 2)
            def _():
                stage_done(slot)

            stage[slot] = (main * (1.0 / divisor_ref[:, at]) + adapter_gain * extra).astype(jnp.bfloat16)
            for b in range(blocks):
                row = plane * plane_rows + b * block_rows
                owner = lax.div(row, own_rows)
                src = stage.at[slot, pl.ds(b * block_rows, block_rows)]
                to = pl.ds(pl.multiple_of(lax.rem(row, own_rows), block_rows), block_rows)
                dst = inbox_ref.at[core, to, at]

                @pl.when(owner == core)
                def _():
                    pltpu.make_async_copy(src, dst, stage_sems.at[slot, b]).start()

                @pl.when(owner != core)
                def _():
                    pltpu.make_async_remote_copy(
                        src_ref=src,
                        dst_ref=dst,
                        send_sem=stage_sems.at[slot, b],
                        recv_sem=inbox_sems.at[core],
                        device_id=(wide, owner),
                        device_id_type=MESH,
                    ).start()
            return 0

        lax.fori_loop(0, tiles, tile_body, 0)
        return 0

    lax.fori_loop(0, n0, plane_body, 0)

    stage_done((n0 * tiles - 2) % 2)
    stage_done((n0 * tiles - 1) % 2)
    for p in range(1, cores):
        sender = lax.rem(core + p, cores)
        part = inbox_ref.at[sender]
        pltpu.make_async_copy(part, part, inbox_sems.at[sender]).wait()

    def sent(count, sem):
        part = gathered_ref.at[pl.ds(0, count)]
        pltpu.make_async_copy(part, part, send_sems.at[sem]).wait()

    for e in range(3):
        each = sends_per_place(e, chains, pieces)
        if chains[e] == 2:
            sent(each, 2 * e)
        elif chains[e] > 2:
            for v in range(chains[e]):
                @pl.when(here[e] == v)
                def _():
                    if v + 1 < chains[e]:
                        sent(each * (v + 1), 2 * e)
                    if v > 0:
                        sent(each * (chains[e] - v), 2 * e + 1)


def shards(
    output_gradient,
    packed_weight_codes,
    group_zero_offsets,
    group_scale_table,
    channel_aware_scale,
    adapter_down_matrix,
    adapter_up_matrix,
):
    wide, cores = lax.axis_size("wide"), lax.axis_size("narrow")
    chains = CHAINS.get(wide, (wide, 1, 1))
    rows, columns = output_gradient.shape
    channels = packed_weight_codes.shape[0]
    rank = adapter_up_matrix.shape[0]
    groups = group_scale_table.shape[0]
    pieces = rows // ROWS
    tokens = rows * wide
    own_rows = tokens // cores
    plane_pieces = chains[1] * chains[2] * pieces
    plane_rows = plane_pieces * ROWS
    blocks = plane_rows // min(plane_rows, own_rows)
    tile = TILE if channels % TILE == 0 else TILE // 2
    dma = pltpu.SemaphoreType.DMA
    any_spec = pl.BlockSpec(memory_space=pl.ANY)
    vmem_spec = pl.BlockSpec(memory_space=pltpu.VMEM)

    def call(*args):
        return kernel(chains, cores, pieces, *args)

    inbox, _ = pl.pallas_call(
        call,
        out_shape=[
            jax.ShapeDtypeStruct((cores, own_rows, channels), jnp.bfloat16),
            jax.ShapeDtypeStruct((wide * pieces, ROWS, columns), jnp.bfloat16),
        ],
        in_specs=[any_spec] * 5 + [vmem_spec] * 2,
        out_specs=[any_spec, any_spec],
        scratch_shapes=[
            pltpu.VMEM((channels, columns), jnp.bfloat16),
            pltpu.VMEM((plane_pieces, ROWS, columns), jnp.bfloat16),
            pltpu.VMEM((WORD_SLOTS, CHUNK, columns // 2), jnp.int32),
            pltpu.VMEM((2, plane_rows, tile), jnp.bfloat16),
            pltpu.VMEM((plane_rows, 2 * rank), jnp.bfloat16),
            pltpu.VMEM((groups, 1, columns), jnp.float32),
            pltpu.VMEM((groups, 1, columns), jnp.float32),
            pltpu.VMEM((groups, columns), jnp.int32),
            pltpu.VMEM((groups, columns), jnp.float32),
            pltpu.VMEM((rank, columns), jnp.bfloat16),
            dma((wide * pieces,)),
            dma((6,)),
            dma,
            dma((3,)),
            dma,
            dma((WORD_SLOTS,)),
            dma((2, blocks)),
            dma((cores,)),
        ],
        compiler_params=pltpu.CompilerParams(
            collective_id=0, has_side_effects=True, vmem_limit_bytes=VMEM_BYTES
        ),
        cost_estimate=pl.CostEstimate(
            flops=2 * tokens * columns * channels,
            bytes_accessed=2 * channels * columns + 6 * tokens * columns,
            transcendentals=0,
        ),
        name="gather_unpack_multiply",
    )(
        output_gradient.reshape(pieces, ROWS, columns),
        packed_weight_codes,
        group_zero_offsets,
        group_scale_table,
        adapter_up_matrix,
        channel_aware_scale.reshape(1, channels),
        adapter_down_matrix.T,
    )
    return add_slots(inbox)


def add_slots(inbox):
    cores, rows, channels = inbox.shape
    block = min(64, rows)

    def body(inbox_ref, out_ref):
        total = inbox_ref[0].astype(jnp.float32)
        for p in range(1, cores):
            total = total + inbox_ref[p].astype(jnp.float32)
        out_ref[...] = total.astype(jnp.bfloat16)

    return pl.pallas_call(
        body,
        out_shape=jax.ShapeDtypeStruct((rows, channels), jnp.bfloat16),
        grid=(rows // block,),
        in_specs=[pl.BlockSpec((cores, block, channels), lambda i: (0, i, 0))],
        out_specs=pl.BlockSpec((block, channels), lambda i: (i, 0)),
        compiler_params=pltpu.CompilerParams(vmem_limit_bytes=32 * 1024 * 1024),
        cost_estimate=pl.CostEstimate(
            flops=cores * rows * channels,
            bytes_accessed=2 * (cores + 1) * rows * channels,
            transcendentals=0,
        ),
        name="add_slots",
    )(inbox)


def solution(mesh):
    placed = (
        P("wide", "narrow"),
        P("wide", "narrow"),
        P("wide", "narrow"),
        P("wide", "narrow"),
        P("wide"),
        P("wide", None),
        P(None, "narrow"),
    )
    return jax.shard_map(
        shards, mesh=mesh, in_specs=placed, out_specs=P("narrow", "wide"), check_vma=False
    )
```

```python
import itertools

import jax
import jax.numpy as jnp
from jax import lax
from jax.experimental import pallas as pl
from jax.experimental.pallas import tpu as pltpu
from jax.sharding import PartitionSpec as P

GROUP = 128
HALF = 128
ROWS = 16
CHUNK = 64
WORD_SLOTS = 3
TILE = 512
VMEM_BYTES = 60 * 1024 * 1024 + 512 * 1024
MESH = pl.DeviceIdType.MESH

adapter_gain = 0.5

CHAINS = {16: (4, 2, 2), 64: (4, 8, 2)}
ORDERS = ((2, 0, 1), (1, 0, 2), (0, 2, 1), (0, 1, 2))


def chain_place(me, i, n):
    lower = 2 * me < n
    low = jnp.where(lower, me, n - 1 - me)
    near = jnp.where(lax.rem(i, 2) == 1, low - lax.div(i + 1, 2), low + lax.div(i, 2))
    place = jnp.where(i <= 2 * low, near, i)
    return jnp.where(lower, place, n - 1 - place)


def earlier(d, e, q, pieces):
    yes = None
    for k in range(min(pieces, len(ORDERS))):
        if ORDERS[k].index(d) < ORDERS[k].index(e):
            hit = lax.rem(q, len(ORDERS)) == k
            yes = hit if yes is None else jnp.logical_or(yes, hit)
    return yes


def arrivals(chains, pieces):
    offsets = list(itertools.product(*map(range, chains)))
    order = sorted(
        ((place, q) for place in offsets[1:] for q in range(pieces)),
        key=lambda event: (sum(event[0]), event[1], event[0]),
    )
    codes = [offsets.index(place) * pieces + q for place, q in order]
    cuts = [
        max([at + 1 for at, (place, _) in enumerate(order) if place[0] <= plane], default=0)
        for plane in range(chains[0])
    ]
    return codes, cuts


def pick(values, at):
    result = jnp.int32(values[0])
    for k in range(1, len(values)):
        result = jnp.where(at == k, jnp.int32(values[k]), result)
    return result


def sends_per_place(e, chains, pieces):
    total = 0
    for q in range(pieces):
        order = ORDERS[q % len(ORDERS)]
        count = 1
        for d in order[: order.index(e)]:
            count *= chains[d]
        total += count
    return total


def kernel(
    chains, cores, pieces,
    own_ref, codes_ref, zero_hbm, scale_hbm, up_hbm, divisor_ref, down_ref,
    inbox_ref, gathered_ref,
    weight, stage, inner, up_ref,
    recv_sems, send_sems, own_sem, table_sems, grads_sems, words_sems, stage_sems, inbox_sems,
):
    wide, core = lax.axis_index("wide"), lax.axis_index("narrow")
    n0, n1, n2 = chains
    strides = (n1 * n2, n2, 1)
    here = (lax.div(wide, n1 * n2), lax.rem(lax.div(wide, n2), n1), lax.rem(wide, n2))
    channels, columns = weight.shape
    plane_pieces = n1 * n2 * pieces
    plane_rows = plane_pieces * ROWS
    own_rows = inbox_ref.shape[1]
    block_rows = min(plane_rows, own_rows)
    blocks = plane_rows // block_rows
    chunks = channels // CHUNK
    tile = stage.shape[2]
    tiles = channels // tile

    own_copy = pltpu.make_async_copy(
        own_ref, gathered_ref.at[pl.ds(wide * pieces, pieces)], own_sem
    )

    def greet():
        barrier = pltpu.get_barrier_semaphore()
        for p in range(1, cores):
            pl.semaphore_signal(
                barrier, inc=1, device_id=(wide, lax.rem(core + p, cores)), device_id_type=MESH
            )
        for e in range(3):
            for step in (1, -1):
                @pl.when((here[e] + step >= 0) & (here[e] + step < chains[e]))
                def _():
                    pl.semaphore_signal(
                        barrier, inc=1, device_id=(wide + step * strides[e], core), device_id_type=MESH
                    )
        greeted = cores - 1
        for e in range(3):
            greeted = greeted + jnp.where(here[e] > 0, 1, 0) + jnp.where(here[e] < chains[e] - 1, 1, 0)
        pl.semaphore_wait(barrier, greeted)

    def forward(src, index, q, offsets, source):
        for e in range(3):
            if chains[e] == 1:
                continue
            clear = jnp.bool_(True)
            for d in range(3):
                if d != e:
                    met = offsets[d] == 0
                    before = earlier(d, e, q, pieces)
                    clear = clear & (met if before is None else met | before)

            def send(ok, step, sem):
                @pl.when(ok)
                def _():
                    pltpu.make_async_remote_copy(
                        src_ref=src,
                        dst_ref=gathered_ref.at[index],
                        send_sem=send_sems.at[sem],
                        recv_sem=recv_sems.at[index],
                        device_id=(wide + step * strides[e], core),
                        device_id_type=MESH,
                    ).start()

            if chains[e] == 2:
                send(clear & (offsets[e] == 0), 1 - 2 * here[e], 2 * e)
            else:
                send(clear & (source[e] <= here[e]) & (here[e] + 1 < chains[e]), 1, 2 * e)
                send(clear & (source[e] >= here[e]) & (here[e] > 0), -1, 2 * e + 1)

    def start_own(q, _):
        forward(own_ref.at[q], wide * pieces + q, q, (0, 0, 0), here)
        return 0

    codes, cuts = arrivals(chains, pieces)
    bits = max(1, (n0 * n1 * n2 * pieces - 1).bit_length())
    per_word = 30 // bits
    packed_codes = [
        sum(code << (bits * k) for k, code in enumerate(codes[at : at + per_word]))
        for at in range(0, len(codes), per_word)
    ]
    first = min(len(codes), cuts[0] + len(codes) // 20)
    done = [max(first, cut) for cut in cuts] + [len(codes)]

    def receive(event, _):
        word = pick(packed_codes, lax.div(event, per_word))
        code = (word >> (lax.rem(event, per_word) * bits)) & ((1 << bits) - 1)
        place, q = lax.div(code, pieces), lax.rem(code, pieces)
        offsets = (lax.div(place, n1 * n2), lax.rem(lax.div(place, n2), n1), lax.rem(place, n2))
        source = tuple(chain_place(here[d], offsets[d], chains[d]) for d in range(3))
        index = (source[0] * strides[0] + source[1] * strides[1] + source[2]) * pieces + q
        slot = gathered_ref.at[index]
        pltpu.make_async_copy(slot, slot, recv_sems.at[index]).wait()
        forward(slot, index, q, offsets, source)
        return 0

    def receive_range(low, high):
        lax.fori_loop(low, high, receive, 0)

    def unpack_all(words, zeros, scales, zero_ref, scale_ref):
        depth = words.shape[0]

        def load_words(c, slot):
            return pltpu.make_async_copy(
                codes_ref.at[pl.ds(pl.multiple_of(c * CHUNK, CHUNK), CHUNK), :],
                words.at[slot],
                words_sems.at[slot],
            )

        for c in range(depth - 1):
            load_words(c, c).start()
        own_copy.start()
        tables = [
            pltpu.make_async_copy(src, dst, table_sems.at[k])
            for k, (src, dst) in enumerate(
                ((zero_hbm, zero_ref), (scale_hbm, scale_ref), (up_hbm, up_ref))
            )
        ]
        for table in tables:
            table.start()

        greet()
        lax.fori_loop(0, pieces, start_own, 0)

        for table in tables:
            table.wait()
        for k in range(zero_ref.shape[0]):
            zeros[k] = zero_ref[k : k + 1, :].astype(jnp.float32)
            scales[k] = scale_ref[k : k + 1, :]

        def unpack(c, _):
            slot = lax.rem(c, depth)

            @pl.when(c + depth - 1 < chunks)
            def _():
                load_words(c + depth - 1, lax.rem(c + depth - 1, depth)).start()

            receive_range(lax.div(c * first, chunks), lax.div((c + 1) * first, chunks))
            load_words(c, slot).wait()
            group = lax.div(c * CHUNK, GROUP)
            rows = pl.ds(pl.multiple_of(c * CHUNK, CHUNK), CHUNK)

            def block(b, _):
                packed = words[slot, :, pl.ds(pl.multiple_of(b * HALF, HALF), HALF)]
                for half, codes in enumerate((packed & 15, packed >> 4)):
                    at = pl.ds(pl.multiple_of(b * 2 * HALF + half * HALF, HALF), HALF)
                    shifted = codes.astype(jnp.float32) - zeros[group, :, at]
                    weight[rows, at] = (shifted * scales[group, :, at]).astype(jnp.bfloat16)
                return 0

            lax.fori_loop(0, columns // (2 * HALF), block, 0, unroll=4)
            return 0

        lax.fori_loop(0, chunks, unpack, 0)

    groups = zero_hbm.shape[0]
    pl.run_scoped(
        unpack_all,
        pltpu.VMEM((WORD_SLOTS, CHUNK, columns // 2), jnp.int32),
        pltpu.VMEM((groups, 1, columns), jnp.float32),
        pltpu.VMEM((groups, 1, columns), jnp.float32),
        pltpu.VMEM((groups, columns), jnp.int32),
        pltpu.VMEM((groups, columns), jnp.float32),
    )
    own_copy.wait()

    def stage_done(slot):
        for b in range(blocks):
            part = stage.at[slot, pl.ds(b * block_rows, block_rows)]
            pltpu.make_async_copy(part, part, stage_sems.at[slot, b]).wait()

    def multiply_all(grads):
        def load_plane(g):
            plane = chain_place(here[0], g, n0)
            return pltpu.make_async_copy(
                gathered_ref.at[pl.ds(plane * plane_pieces, plane_pieces)],
                grads.at[lax.rem(g, 2)],
                grads_sems.at[lax.rem(g, 2)],
            )

        def plane_body(g, _):
            plane = chain_place(here[0], g, n0)
            held = lax.rem(g, 2)
            load_plane(g).wait()
            up = up_ref[...]
            sums = lax.dot_general(
                grads[held].reshape(plane_rows, columns),
                jnp.concatenate([up, up], axis=0),
                (((1,), (1,)), ((), ())),
                preferred_element_type=jnp.float32,
            )
            high = sums.astype(jnp.bfloat16)
            rest = (sums - high.astype(jnp.float32)).astype(jnp.bfloat16)
            rank = up_ref.shape[0]
            lane = lax.broadcasted_iota(jnp.int32, sums.shape, 1)
            inner[...] = jnp.where(lane < rank, high.astype(jnp.float32), rest.astype(jnp.float32)).astype(jnp.bfloat16)
            low, events = pick(done, g), pick(done, g + 1) - pick(done, g)

            def tile_body(j, _):
                receive_range(low + lax.div(j * events, tiles), low + lax.div((j + 1) * events, tiles))

                @pl.when((j == tiles - 1) & (g + 1 < n0))
                def _():
                    load_plane(g + 1).start()

                count = g * tiles + j
                slot = lax.rem(count, 2)
                at = pl.ds(pl.multiple_of(j * tile, tile), tile)
                main = lax.dot_general(
                    weight[at, :],
                    grads[held].reshape(plane_rows, columns),
                    (((1,), (1,)), ((), ())),
                    preferred_element_type=jnp.float32,
                ).T
                down = down_ref[:, at]
                extra = jnp.dot(
                    inner[...], jnp.concatenate([down, down], axis=0), preferred_element_type=jnp.float32
                )

                @pl.when(count >= 2)
                def _():
                    stage_done(slot)

                stage[slot] = (main * (1.0 / divisor_ref[:, at]) + adapter_gain * extra).astype(jnp.bfloat16)
                for b in range(blocks):
                    row = plane * plane_rows + b * block_rows
                    owner = lax.div(row, own_rows)
                    src = stage.at[slot, pl.ds(b * block_rows, block_rows)]
                    to = pl.ds(pl.multiple_of(lax.rem(row, own_rows), block_rows), block_rows)
                    dst = inbox_ref.at[core, to, at]

                    @pl.when(owner == core)
                    def _():
                        pltpu.make_async_copy(src, dst, stage_sems.at[slot, b]).start()

                    @pl.when(owner != core)
                    def _():
                        pltpu.make_async_remote_copy(
                            src_ref=src,
                            dst_ref=dst,
                            send_sem=stage_sems.at[slot, b],
                            recv_sem=inbox_sems.at[core],
                            device_id=(wide, owner),
                            device_id_type=MESH,
                        ).start()
                return 0

            lax.fori_loop(0, tiles, tile_body, 0)
            return 0

        load_plane(0).start()
        lax.fori_loop(0, n0, plane_body, 0)

    pl.run_scoped(multiply_all, pltpu.VMEM((2, plane_pieces, ROWS, columns), jnp.bfloat16))

    stage_done((n0 * tiles - 2) % 2)
    stage_done((n0 * tiles - 1) % 2)
    for p in range(1, cores):
        sender = lax.rem(core + p, cores)
        part = inbox_ref.at[sender]
        pltpu.make_async_copy(part, part, inbox_sems.at[sender]).wait()

    def sent(count, sem):
        part = gathered_ref.at[pl.ds(0, count)]
        pltpu.make_async_copy(part, part, send_sems.at[sem]).wait()

    for e in range(3):
        each = sends_per_place(e, chains, pieces)
        if chains[e] == 2:
            sent(each, 2 * e)
        elif chains[e] > 2:
            for v in range(chains[e]):
                @pl.when(here[e] == v)
                def _():
                    if v + 1 < chains[e]:
                        sent(each * (v + 1), 2 * e)
                    if v > 0:
                        sent(each * (chains[e] - v), 2 * e + 1)


def shards(
    output_gradient,
    packed_weight_codes,
    group_zero_offsets,
    group_scale_table,
    channel_aware_scale,
    adapter_down_matrix,
    adapter_up_matrix,
):
    wide, cores = lax.axis_size("wide"), lax.axis_size("narrow")
    chains = CHAINS.get(wide, (wide, 1, 1))
    rows, columns = output_gradient.shape
    channels = packed_weight_codes.shape[0]
    rank = adapter_up_matrix.shape[0]
    pieces = rows // ROWS
    tokens = rows * wide
    own_rows = tokens // cores
    plane_pieces = chains[1] * chains[2] * pieces
    plane_rows = plane_pieces * ROWS
    blocks = plane_rows // min(plane_rows, own_rows)
    tile = TILE if channels % TILE == 0 else TILE // 2
    dma = pltpu.SemaphoreType.DMA
    any_spec = pl.BlockSpec(memory_space=pl.ANY)
    vmem_spec = pl.BlockSpec(memory_space=pltpu.VMEM)

    def call(*args):
        return kernel(chains, cores, pieces, *args)

    inbox, _ = pl.pallas_call(
        call,
        out_shape=[
            jax.ShapeDtypeStruct((cores, own_rows, channels), jnp.bfloat16),
            jax.ShapeDtypeStruct((wide * pieces, ROWS, columns), jnp.bfloat16),
        ],
        in_specs=[any_spec] * 5 + [vmem_spec] * 2,
        out_specs=[any_spec, any_spec],
        scratch_shapes=[
            pltpu.VMEM((channels, columns), jnp.bfloat16),
            pltpu.VMEM((2, plane_rows, tile), jnp.bfloat16),
            pltpu.VMEM((plane_rows, 2 * rank), jnp.bfloat16),
            pltpu.VMEM((rank, columns), jnp.bfloat16),
            dma((wide * pieces,)),
            dma((6,)),
            dma,
            dma((3,)),
            dma((2,)),
            dma((WORD_SLOTS,)),
            dma((2, blocks)),
            dma((cores,)),
        ],
        compiler_params=pltpu.CompilerParams(
            collective_id=0, has_side_effects=True, vmem_limit_bytes=VMEM_BYTES
        ),
        cost_estimate=pl.CostEstimate(
            flops=2 * tokens * columns * channels,
            bytes_accessed=2 * channels * columns + 6 * tokens * columns,
            transcendentals=0,
        ),
        name="gather_unpack_multiply",
    )(
        output_gradient.reshape(pieces, ROWS, columns),
        packed_weight_codes,
        group_zero_offsets,
        group_scale_table,
        adapter_up_matrix,
        channel_aware_scale.reshape(1, channels),
        adapter_down_matrix.T,
    )
    return add_slots(inbox)


def add_slots(inbox):
    cores, rows, channels = inbox.shape
    block = min(64, rows)

    def body(inbox_ref, out_ref):
        total = inbox_ref[0].astype(jnp.float32)
        for p in range(1, cores):
            total = total + inbox_ref[p].astype(jnp.float32)
        out_ref[...] = total.astype(jnp.bfloat16)

    return pl.pallas_call(
        body,
        out_shape=jax.ShapeDtypeStruct((rows, channels), jnp.bfloat16),
        grid=(rows // block,),
        in_specs=[pl.BlockSpec((cores, block, channels), lambda i: (0, i, 0))],
        out_specs=pl.BlockSpec((block, channels), lambda i: (i, 0)),
        compiler_params=pltpu.CompilerParams(vmem_limit_bytes=VMEM_BYTES),
        cost_estimate=pl.CostEstimate(
            flops=cores * rows * channels,
            bytes_accessed=2 * (cores + 1) * rows * channels,
            transcendentals=0,
        ),
        name="add_slots",
    )(inbox)


def solution(mesh):
    placed = (
        P("wide", "narrow"),
        P("wide", "narrow"),
        P("wide", "narrow"),
        P("wide", "narrow"),
        P("wide"),
        P("wide", None),
        P(None, "narrow"),
    )
    return jax.shard_map(
        shards, mesh=mesh, in_specs=placed, out_specs=P("narrow", "wide"), check_vma=False
    )
```
